32 devices in a mesh: dp: 4 (over x, core), mx: 4 (over z), my: 2 (over y).
Axes of the slice: x: 2, y: 2, z: 4, core: 2. Of those that a mesh axis runs over, the one named last changes fastest.
Arguments:
- tokens: bfloat16 [1024, 6144], P('dp', ('mx', 'my')), may hold values from -6 to 6
- cotangent: bfloat16 [1024, 6144], P('dp', ('mx', 'my')), may hold values from -1.1953125 to 1.1953125
- w_in: bfloat16 [6144, 12288], P('mx', 'my'), may hold values from -0.078125 to 0.078125
- w_out: bfloat16 [12288, 6144], P('my', 'mx'), may hold values from -0.0546875 to 0.0546875
Outputs:
- output: bfloat16 [1024, 6144], P('dp', ('mx', 'my'))
- input_grad: bfloat16 [1024, 6144], P('dp', ('mx', 'my'))
- w_in_grad: bfloat16 [6144, 12288], P('mx', ('my', 'dp'))
- w_out_grad: bfloat16 [12288, 6144], P(('my', 'dp'), 'mx')
The draws below stay inside these ranges and needn't reach their ends.
All inputs are finite; a program needn't handle non-finite values.
Results may differ from the reference program's by a relative error of at most 0.019.
Values may be sent and summed in bfloat16 or wider, within the bound.
A program may use at most 192 MiB of HBM per device.

```python
import jax
import jax.numpy as jnp
from jax import lax

D = 6144
FF = 12288
TOK_DEV = 256
TOKENS = 1024
N_DP = 4
N_MY = 2


def levels(stream_key, extent, shards, least, high):
    level, own = 1.0, jax.random.fold_in(stream_key, 6)
    for position, parts in shards:
        steps = jnp.exp(jax.random.uniform(jax.random.fold_in(own, position), (parts,), jnp.float32, least / len(shards), high / len(shards)))
        level = level * jnp.repeat(steps, extent[position] // parts).reshape([-1 if axis == position else 1 for axis in range(len(extent))])
    return level


def scatter_about(rng, shape, deviation, reach, pieces=(), held_as=jnp.bfloat16):
    factor_of = levels(rng, shape, pieces, -0.22, 0.18) if pieces else 1.0
    array = jax.random.normal(rng, shape, jnp.float32) * deviation * factor_of
    return jnp.minimum(jnp.maximum(array, -reach), reach).astype(held_as)


def setup_inputs(seed: int = 0) -> dict:
    streams_of = jax.random.split(jax.random.key(seed), 5)
    tokens = scatter_about(streams_of[0], (TOKENS, D), 1.0, 6.0, ((0, 4), (1, 8)))
    cotangent = scatter_about(streams_of[1], (TOKENS, D), 0.2, 1.1953125, ((0, 4), (1, 8)))
    w_in = scatter_about(streams_of[2], (D, FF), D ** -0.5, 0.078125, ((0, 4), (1, 2)))
    w_out = scatter_about(streams_of[3], (FF, D), FF ** -0.5, 0.0546875, ((0, 2), (1, 4)))
    return {"tokens": tokens, "cotangent": cotangent, "w_in": w_in, "w_out": w_out}


def gelu_parts(hidden):
    cdf = 0.5 * (1.0 + lax.erf(hidden * 0.7071067811865476))
    density = jnp.exp(-0.5 * hidden * hidden) * 0.3989422804014327
    return hidden * cdf, cdf + hidden * density


def rounded(value):
    return lax.optimization_barrier(value.astype(jnp.bfloat16)).astype(jnp.float32)


def block_sum(left, right):
    width = FF // N_MY
    left_blocks = left.reshape(left.shape[0], N_MY, width).transpose(1, 0, 2)
    right_blocks = right.reshape(N_MY, width, right.shape[1])

    def step(carry, pair):
        part = jnp.dot(pair[0], pair[1], preferred_element_type=jnp.float32)
        return carry + rounded(part), None

    start = jnp.zeros((left.shape[0], right.shape[1]), jnp.float32)
    summed, unused = lax.scan(step, start, (left_blocks, right_blocks))
    return summed


def token_sum(left, right):
    left_blocks = left.reshape(N_DP, TOK_DEV, left.shape[1])
    right_blocks = right.reshape(N_DP, TOK_DEV, right.shape[1])

    def step(carry, pair):
        part = lax.dot_general(pair[0], pair[1], (((0,), (0,)), ((), ())), preferred_element_type=jnp.float32)
        return carry + rounded(part), None

    start = jnp.zeros((left.shape[1], right.shape[1]), jnp.float32)
    summed, unused = lax.scan(step, start, (left_blocks, right_blocks))
    return summed


def reference(tokens, cotangent, w_in, w_out):
    hidden = jnp.dot(tokens, w_in, preferred_element_type=jnp.float32)
    act_full, slope = gelu_parts(hidden)
    active = act_full.astype(jnp.bfloat16)
    output = block_sum(active, w_out).astype(jnp.bfloat16)
    act_grad = jnp.dot(cotangent, w_out.T, preferred_element_type=jnp.float32)
    hidden_grad = (act_grad * slope).astype(jnp.bfloat16)
    input_grad = block_sum(hidden_grad, w_in.T).astype(jnp.bfloat16)
    w_in_grad = token_sum(tokens, hidden_grad).astype(jnp.bfloat16)
    w_out_grad = token_sum(active, cotangent).astype(jnp.bfloat16)
    return output, input_grad, w_in_grad, w_out_grad
```

```python
import jax
import jax.numpy as jnp
from jax import lax
from jax.sharding import PartitionSpec as P


def gelu_parts(hidden):
    cdf = 0.5 * (1.0 + lax.erf(hidden * 0.7071067811865476))
    density = jnp.exp(-0.5 * hidden * hidden) * 0.3989422804014327
    return (hidden * cdf, cdf + hidden * density)


def mm(a, b, ca, cb):
    return lax.dot_general(
        a, b, (((ca,), (cb,)), ((), ())), preferred_element_type=jnp.float32
    ).astype(jnp.bfloat16)


def per_device(tokens, cotangent, w_in, w_out):
    n_dp = lax.axis_size("dp")
    width = w_in.shape[1] // n_dp
    start = lax.axis_index("dp") * width
    win = lax.dynamic_slice_in_dim(w_in, start, width, 1)
    wout = lax.dynamic_slice_in_dim(w_out, start, width, 0)

    def gather(x):
        x = lax.all_gather(x, "my", axis=1, tiled=True)
        return lax.all_gather(x, "dp", axis=0, tiled=True)

    def scatter(x):
        x = lax.psum_scatter(x, "dp", scatter_dimension=0, tiled=True)
        return lax.psum_scatter(x, "my", scatter_dimension=1, tiled=True)

    toks = gather(tokens)
    cots = gather(cotangent)
    hidden = lax.psum_scatter(mm(toks, win, 1, 0), "mx", scatter_dimension=0, tiled=True)
    act_grad = lax.psum_scatter(mm(cots, wout, 1, 1), "mx", scatter_dimension=0, tiled=True)
    act_full, slope = gelu_parts(hidden.astype(jnp.float32))
    active = act_full.astype(jnp.bfloat16)
    hidden_grad = (act_grad.astype(jnp.float32) * slope).astype(jnp.bfloat16)
    active = lax.all_gather(active, "mx", axis=0, tiled=True)
    hidden_grad = lax.all_gather(hidden_grad, "mx", axis=0, tiled=True)
    output = scatter(mm(active, wout, 1, 0))
    input_grad = scatter(mm(hidden_grad, win, 1, 1))
    w_out_grad = mm(active, cots, 0, 0)
    w_in_grad = mm(toks, hidden_grad, 0, 0)
    return (output, input_grad, w_in_grad, w_out_grad)


def solution(mesh):
    in_specs = (P("dp", ("mx", "my")), P("dp", ("mx", "my")), P("mx", "my"), P("my", "mx"))
    out_specs = (
        P("dp", ("mx", "my")),
        P("dp", ("mx", "my")),
        P("mx", ("my", "dp")),
        P(("my", "dp"), "mx"),
    )
    return jax.shard_map(
        per_device, mesh=mesh, in_specs=in_specs, out_specs=out_specs, check_vma=False
    )
```

```python
import functools

import jax
import jax.numpy as jnp
from jax import lax
from jax.experimental import pallas as pl
from jax.experimental.pallas import tpu as pltpu
from jax.sharding import PartitionSpec as P


def gelu_parts(hidden):
    cdf = 0.5 * (1.0 + lax.erf(hidden * 0.7071067811865476))
    density = jnp.exp(-0.5 * hidden * hidden) * 0.3989422804014327
    return (hidden * cdf, cdf + hidden * density)


def mm(a, b, ca, cb):
    return lax.dot_general(
        a, b, (((ca,), (cb,)), ((), ())), preferred_element_type=jnp.float32
    ).astype(jnp.bfloat16)


MESH = pl.DeviceIdType.MESH
TILE = 256
SKEW = 2


def dot(a, b, ca, cb):
    return lax.dot_general(a, b, (((ca,), (cb,)), ((), ())), preferred_element_type=jnp.float32)


def kernel(
    n, tok_ref, cot_ref, win_hbm, wout_hbm, out_ref, toks_hbm, cots_hbm, acts_hbm,
    win, wout, toks, cots, sums, acts, parts, landed,
    local_sem, gat_send, gat_recv, rs_send, rs_recv, ag_send, ag_recv, out_send, out_recv,
):
    dp, z, my = lax.axis_index("dp"), lax.axis_index("mx"), lax.axis_index("my")
    x, c = dp // 2, dp % 2
    rows, width = tok_ref.shape
    hidden = win.shape[1]
    half = hidden // 2
    per_half = half // TILE
    steps = 4 * per_half
    lag = (n - 1) * SKEW

    def block_of(j):
        return ((x + ((j + 1) // 2) % 2) % 2) * 2 + (c + j // 2) % 2

    def row_slice(t):
        return pl.ds(pl.multiple_of(t * rows, rows), rows)

    def col_slice(m):
        return pl.ds(pl.multiple_of(m * width, width), width)

    peers = []
    for co, xo, yo in ((0, 0, 1), (0, 1, 0), (0, 1, 1), (1, 1, 0), (1, 1, 1), (1, 0, 0), (1, 0, 1)):
        peers.append((((x + xo) % 2) * 2 + (c + co) % 2, (my + yo) % 2))

    cut = pl.ds(pl.multiple_of(dp * hidden, hidden), hidden)
    loads = [
        pltpu.make_async_copy(win_hbm.at[:, cut], win, local_sem.at[0]),
        pltpu.make_async_copy(wout_hbm.at[cut, :], wout, local_sem.at[1]),
        pltpu.make_async_copy(tok_ref, toks.at[row_slice(dp), col_slice(my)], local_sem.at[2]),
        pltpu.make_async_copy(cot_ref, cots.at[row_slice(dp), col_slice(my)], local_sem.at[3]),
    ]
    for load in loads:
        load.start()

    barrier = pltpu.get_barrier_semaphore()
    for pd, pm in peers:
        pl.semaphore_signal(barrier, inc=1, device_id=(pd, z, pm), device_id_type=MESH)

    @pl.when(z > 0)
    def _():
        pl.semaphore_signal(barrier, inc=1, device_id=(dp, z - 1, my), device_id_type=MESH)

    @pl.when(z < n - 1)
    def _():
        pl.semaphore_signal(barrier, inc=1, device_id=(dp, z + 1, my), device_id_type=MESH)

    pl.semaphore_wait(barrier, 7 + jnp.where(z > 0, 1, 0) + jnp.where(z < n - 1, 1, 0))

    def gather_copy(k, src_ref, dst, source, target):
        return pltpu.make_async_remote_copy(
            src_ref=src_ref,
            dst_ref=dst.at[row_slice(source[0]), col_slice(source[1])],
            send_sem=gat_send.at[k, target[0] * 2 + target[1]],
            recv_sem=gat_recv.at[k, source[0] * 2 + source[1]],
            device_id=(target[0], z, target[1]),
            device_id_type=MESH,
        )

    for peer in peers:
        gather_copy(0, tok_ref, toks, (dp, my), peer).start()
        gather_copy(1, cot_ref, cots, (dp, my), peer).start()

    def tile_of(d, idx):
        t = block_of(idx // per_half)
        first = pl.multiple_of(d * half + (idx % per_half) * TILE, TILE)
        return row_slice(t), pl.ds(first, TILE)

    def chain_copy(buf, sends, recvs, d, idx, target):
        r, f = tile_of(d, idx)
        return pltpu.make_async_remote_copy(
            src_ref=buf.at[:, r, f],
            dst_ref=buf.at[:, r, f],
            send_sem=sends.at[d, idx],
            recv_sem=recvs.at[d, idx],
            device_id=(dp, target, my),
            device_id_type=MESH,
        )

    def out_copy(t, m, source, target):
        return pltpu.make_async_remote_copy(
            src_ref=parts.at[:, row_slice(t), col_slice(m)],
            dst_ref=landed.at[:, source[0] * 2 + source[1]],
            send_sem=out_send.at[t * 2 + m],
            recv_sem=out_recv.at[source[0] * 2 + source[1]],
            device_id=(target[0], z, target[1]),
            device_id_type=MESH,
        )

    for load in loads:
        load.wait()

    nearest = jnp.minimum(z, n - 1 - z)

    @pl.loop(0, steps + 2 * lag)
    def _(s):
        lead = s - nearest * SKEW

        @pl.when((lead >= 0) & (lead < steps) & (lead % per_half == 0))
        def _():
            t = block_of(lead // per_half)
            for m in range(2):
                @pl.when((t != dp) | (my != m))
                def _():
                    gather_copy(0, tok_ref, toks, (t, m), (dp, my)).wait_recv()
                    gather_copy(1, cot_ref, cots, (t, m), (dp, my)).wait_recv()

        for d in range(2):
            pos = z if d == 0 else n - 1 - z
            ahead = z + 1 if d == 0 else z - 1
            behind = z - 1 if d == 0 else z + 1
            idx = s - pos * SKEW

            @pl.when((idx >= 0) & (idx < steps))
            def _():
                r, f = tile_of(d, idx)
                h = dot(toks[r, :], win[:, f], 1, 0)
                a = dot(cots[r, :], wout[f, :], 1, 1)

                @pl.when(pos == 0)
                def _():
                    sums[0, r, f] = h.astype(jnp.bfloat16)
                    sums[1, r, f] = a.astype(jnp.bfloat16)
                    chain_copy(sums, rs_send, rs_recv, d, idx, ahead).start()

                @pl.when((pos > 0) & (pos < n - 1))
                def _():
                    chain_copy(sums, rs_send, rs_recv, d, idx, ahead).wait_recv()
                    sums[0, r, f] = (sums[0, r, f].astype(jnp.float32) + h).astype(jnp.bfloat16)
                    sums[1, r, f] = (sums[1, r, f].astype(jnp.float32) + a).astype(jnp.bfloat16)
                    chain_copy(sums, rs_send, rs_recv, d, idx, ahead).start()

                @pl.when(pos == n - 1)
                def _():
                    chain_copy(sums, rs_send, rs_recv, d, idx, behind).wait_recv()
                    hs = sums[0, r, f].astype(jnp.float32) + h
                    grad = sums[1, r, f].astype(jnp.float32) + a
                    act_full, slope = gelu_parts(hs)
                    acts[0, r, f] = act_full.astype(jnp.bfloat16)
                    acts[1, r, f] = (grad * slope).astype(jnp.bfloat16)
                    chain_copy(acts, ag_send, ag_recv, d, idx, behind).start()

            back = s - lag - (n - 1 - pos) * SKEW

            @pl.when((back >= 0) & (back < steps) & (pos < n - 1))
            def _():
                chain_copy(acts, ag_send, ag_recv, d, back, ahead).wait_recv()

                @pl.when(pos > 0)
                def _():
                    chain_copy(acts, ag_send, ag_recv, d, back, behind).start()

        done = s - 2 * lag

        @pl.when((done >= 0) & (done % per_half == per_half - 1))
        def _():
            t = block_of(done // per_half)
            r = row_slice(t)
            parts[0, r, :] = dot(acts[0, r, :], wout[...], 1, 0).astype(jnp.bfloat16)
            parts[1, r, :] = dot(acts[1, r, :], win[...], 1, 1).astype(jnp.bfloat16)
            for m in range(2):
                @pl.when((t != dp) | (my != m))
                def _():
                    out_copy(t, m, (dp, my), (t, m)).start()

    stores = [
        pltpu.make_async_copy(toks, toks_hbm, local_sem.at[0]),
        pltpu.make_async_copy(cots, cots_hbm, local_sem.at[1]),
        pltpu.make_async_copy(acts, acts_hbm, local_sem.at[2]),
    ]
    for store in stores:
        store.start()

    for d in range(2):
        pos = z if d == 0 else n - 1 - z

        @pl.loop(0, steps)
        def _(idx):
            other = jnp.where(z == 0, 1, z - 1)

            @pl.when(pos < n - 1)
            def _():
                chain_copy(sums, rs_send, rs_recv, d, idx, other).wait_send()

            @pl.when(pos > 0)
            def _():
                chain_copy(acts, ag_send, ag_recv, d, idx, other).wait_send()

    for peer in peers:
        gather_copy(0, tok_ref, toks, (dp, my), peer).wait_send()
        gather_copy(1, cot_ref, cots, (dp, my), peer).wait_send()

    out_ref[...] = parts[:, row_slice(dp), col_slice(my)].astype(jnp.float32)
    for peer in peers:
        out_copy(dp, my, peer, peer).wait_recv()
        out_ref[...] += landed[:, peer[0] * 2 + peer[1]].astype(jnp.float32)
    for peer in peers:
        out_copy(peer[0], peer[1], (dp, my), peer).wait_send()
    for store in stores:
        store.wait()


def fused(tokens, cotangent, w_in, w_out):
    n = lax.axis_size("mx")
    rows, width = tokens.shape
    hidden = w_in.shape[1] // 4
    deep = w_in.shape[0]
    bf16 = jnp.bfloat16
    steps = 4 * (hidden // 2 // TILE)
    vmem = pl.BlockSpec(memory_space=pltpu.VMEM)
    hbm = pl.BlockSpec(memory_space=pl.ANY)
    dma = pltpu.SemaphoreType.DMA
    outs, toks, cots, acts = pl.pallas_call(
        functools.partial(kernel, n),
        out_shape=(
            jax.ShapeDtypeStruct((2, rows, width), jnp.float32),
            jax.ShapeDtypeStruct((4 * rows, deep), bf16),
            jax.ShapeDtypeStruct((4 * rows, deep), bf16),
            jax.ShapeDtypeStruct((2, 4 * rows, hidden), bf16),
        ),
        in_specs=[vmem, vmem, hbm, hbm],
        out_specs=(vmem, hbm, hbm, hbm),
        scratch_shapes=[
            pltpu.VMEM((deep, hidden), bf16),
            pltpu.VMEM((hidden, deep), bf16),
            pltpu.VMEM((4 * rows, deep), bf16),
            pltpu.VMEM((4 * rows, deep), bf16),
            pltpu.VMEM((2, 4 * rows, hidden), bf16),
            pltpu.VMEM((2, 4 * rows, hidden), bf16),
            pltpu.VMEM((2, 4 * rows, deep), bf16),
            pltpu.VMEM((2, 8, rows, width), bf16),
            dma((4,)),
            dma((2, 8)),
            dma((2, 8)),
            dma((2, steps)),
            dma((2, steps)),
            dma((2, steps)),
            dma((2, steps)),
            dma((8,)),
            dma((8,)),
        ],
        compiler_params=pltpu.CompilerParams(
            collective_id=0, has_side_effects=True, vmem_limit_bytes=60 * 2**20
        ),
        cost_estimate=pl.CostEstimate(
            flops=16 * rows * hidden * deep * 2, bytes_accessed=4 * hidden * deep, transcendentals=0
        ),
    )(tokens, cotangent, w_in, w_out)
    return (
        outs[0].astype(bf16),
        outs[1].astype(bf16),
        mm(toks, acts[1], 0, 0),
        mm(acts[0], cots, 0, 0),
    )


def per_device(tokens, cotangent, w_in, w_out):
    n_dp = lax.axis_size("dp")
    aligned = tokens.shape[0] % 16 == 0 and tokens.shape[1] % 128 == 0
    aligned = aligned and w_in.shape[1] % (8 * TILE) == 0
    if n_dp == 4 and lax.axis_size("my") == 2 and lax.axis_size("mx") > 1 and aligned:
        return fused(tokens, cotangent, w_in, w_out)
    width = w_in.shape[1] // n_dp
    start = lax.axis_index("dp") * width
    win = lax.dynamic_slice_in_dim(w_in, start, width, 1)
    wout = lax.dynamic_slice_in_dim(w_out, start, width, 0)

    def gather(x):
        x = lax.all_gather(x, "my", axis=1, tiled=True)
        return lax.all_gather(x, "dp", axis=0, tiled=True)

    def scatter(x):
        x = lax.psum_scatter(x, "dp", scatter_dimension=0, tiled=True)
        return lax.psum_scatter(x, "my", scatter_dimension=1, tiled=True)

    toks = gather(tokens)
    cots = gather(cotangent)
    hidden = lax.psum_scatter(mm(toks, win, 1, 0), "mx", scatter_dimension=0, tiled=True)
    act_grad = lax.psum_scatter(mm(cots, wout, 1, 1), "mx", scatter_dimension=0, tiled=True)
    act_full, slope = gelu_parts(hidden.astype(jnp.float32))
    active = act_full.astype(jnp.bfloat16)
    hidden_grad = (act_grad.astype(jnp.float32) * slope).astype(jnp.bfloat16)
    active = lax.all_gather(active, "mx", axis=0, tiled=True)
    hidden_grad = lax.all_gather(hidden_grad, "mx", axis=0, tiled=True)
    output = scatter(mm(active, wout, 1, 0))
    input_grad = scatter(mm(hidden_grad, win, 1, 1))
    w_out_grad = mm(active, cots, 0, 0)
    w_in_grad = mm(toks, hidden_grad, 0, 0)
    return (output, input_grad, w_in_grad, w_out_grad)


def solution(mesh):
    in_specs = (P("dp", ("mx", "my")), P("dp", ("mx", "my")), P("mx", "my"), P("my", "mx"))
    out_specs = (
        P("dp", ("mx", "my")),
        P("dp", ("mx", "my")),
        P("mx", ("my", "dp")),
        P(("my", "dp"), "mx"),
    )
    return jax.shard_map(
        per_device, mesh=mesh, in_specs=in_specs, out_specs=out_specs, check_vma=False
    )
```

```python
import functools

import jax
import jax.numpy as jnp
from jax import lax
from jax.experimental import pallas as pl
from jax.experimental.pallas import tpu as pltpu
from jax.sharding import PartitionSpec as P


def gelu_parts(hidden):
    cdf = 0.5 * (1.0 + lax.erf(hidden * 0.7071067811865476))
    density = jnp.exp(-0.5 * hidden * hidden) * 0.3989422804014327
    return (hidden * cdf, cdf + hidden * density)


def mm(a, b, ca, cb):
    return lax.dot_general(
        a, b, (((ca,), (cb,)), ((), ())), preferred_element_type=jnp.float32
    ).astype(jnp.bfloat16)


MESH = pl.DeviceIdType.MESH
TILE = 128
SKEW = 1


def dot(a, b, ca, cb):
    return lax.dot_general(a, b, (((ca,), (cb,)), ((), ())), preferred_element_type=jnp.float32)


def kernel(
    n, tok_ref, cot_ref, win_hbm, wout_hbm, out_ref, toks_hbm, cots_hbm, acts_hbm,
    win, wout, toks, cots, sums, acts, parts, landed,
    local_sem, gat_send, gat_recv, rs_send, rs_recv, ag_send, ag_recv, out_send, out_recv,
):
    dp, z, my = lax.axis_index("dp"), lax.axis_index("mx"), lax.axis_index("my")
    x, c = dp // 2, dp % 2
    rows, width = tok_ref.shape
    hidden = win.shape[1]
    half = hidden // 2
    per_half = half // TILE
    steps = 4 * per_half
    lag = (n - 1) * SKEW

    def block_of(j):
        return ((x + ((j + 1) // 2) % 2) % 2) * 2 + (c + j // 2) % 2

    def row_slice(t):
        return pl.ds(pl.multiple_of(t * rows, rows), rows)

    def col_slice(m):
        return pl.ds(pl.multiple_of(m * width, width), width)

    peers = []
    for co, xo, yo in ((0, 0, 1), (0, 1, 0), (0, 1, 1), (1, 1, 0), (1, 1, 1), (1, 0, 0), (1, 0, 1)):
        peers.append((((x + xo) % 2) * 2 + (c + co) % 2, (my + yo) % 2))

    cut = pl.ds(pl.multiple_of(dp * hidden, hidden), hidden)
    loads = [
        pltpu.make_async_copy(win_hbm.at[:, cut], win, local_sem.at[0]),
        pltpu.make_async_copy(wout_hbm.at[cut, :], wout, local_sem.at[1]),
        pltpu.make_async_copy(tok_ref, toks.at[row_slice(dp), col_slice(my)], local_sem.at[2]),
        pltpu.make_async_copy(cot_ref, cots.at[row_slice(dp), col_slice(my)], local_sem.at[3]),
    ]
    for load in loads:
        load.start()

    barrier = pltpu.get_barrier_semaphore()
    for pd, pm in peers:
        pl.semaphore_signal(barrier, inc=1, device_id=(pd, z, pm), device_id_type=MESH)

    @pl.when(z > 0)
    def _():
        pl.semaphore_signal(barrier, inc=1, device_id=(dp, z - 1, my), device_id_type=MESH)

    @pl.when(z < n - 1)
    def _():
        pl.semaphore_signal(barrier, inc=1, device_id=(dp, z + 1, my), device_id_type=MESH)

    pl.semaphore_wait(barrier, 7 + jnp.where(z > 0, 1, 0) + jnp.where(z < n - 1, 1, 0))

    def gather_copy(k, src_ref, dst, source, target):
        return pltpu.make_async_remote_copy(
            src_ref=src_ref,
            dst_ref=dst.at[row_slice(source[0]), col_slice(source[1])],
            send_sem=gat_send.at[k, target[0] * 2 + target[1]],
            recv_sem=gat_recv.at[k, source[0] * 2 + source[1]],
            device_id=(target[0], z, target[1]),
            device_id_type=MESH,
        )

    for peer in peers:
        gather_copy(0, tok_ref, toks, (dp, my), peer).start()
        gather_copy(1, cot_ref, cots, (dp, my), peer).start()

    def tile_of(d, idx):
        t = block_of(idx // per_half)
        first = pl.multiple_of(d * half + (idx % per_half) * TILE, TILE)
        return row_slice(t), pl.ds(first, TILE)

    def chain_copy(buf, sends, recvs, d, idx, target):
        r, f = tile_of(d, idx)
        return pltpu.make_async_remote_copy(
            src_ref=buf.at[:, r, f],
            dst_ref=buf.at[:, r, f],
            send_sem=sends.at[d, idx],
            recv_sem=recvs.at[d, idx],
            device_id=(dp, target, my),
            device_id_type=MESH,
        )

    def out_copy(t, m, source, target):
        return pltpu.make_async_remote_copy(
            src_ref=parts.at[:, row_slice(t), col_slice(m)],
            dst_ref=landed.at[:, source[0] * 2 + source[1]],
            send_sem=out_send.at[t * 2 + m],
            recv_sem=out_recv.at[source[0] * 2 + source[1]],
            device_id=(target[0], z, target[1]),
            device_id_type=MESH,
        )

    for load in loads:
        load.wait()

    nearest = jnp.minimum(z, n - 1 - z)

    @pl.loop(0, steps + 2 * lag)
    def _(s):
        lead = s - nearest * SKEW

        @pl.when((lead >= 0) & (lead < steps) & (lead % per_half == 0))
        def _():
            t = block_of(lead // per_half)
            for m in range(2):
                @pl.when((t != dp) | (my != m))
                def _():
                    gather_copy(0, tok_ref, toks, (t, m), (dp, my)).wait_recv()
                    gather_copy(1, cot_ref, cots, (t, m), (dp, my)).wait_recv()

        for d in range(2):
            pos = z if d == 0 else n - 1 - z
            ahead = z + 1 if d == 0 else z - 1
            behind = z - 1 if d == 0 else z + 1
            idx = s - pos * SKEW

            @pl.when((idx >= 0) & (idx < steps))
            def _():
                r, f = tile_of(d, idx)
                h = dot(toks[r, :], win[:, f], 1, 0)
                a = dot(cots[r, :], wout[f, :], 1, 1)

                @pl.when(pos == 0)
                def _():
                    sums[0, r, f] = h.astype(jnp.bfloat16)
                    sums[1, r, f] = a.astype(jnp.bfloat16)
                    chain_copy(sums, rs_send, rs_recv, d, idx, ahead).start()

                @pl.when((pos > 0) & (pos < n - 1))
                def _():
                    chain_copy(sums, rs_send, rs_recv, d, idx, ahead).wait_recv()
                    sums[0, r, f] = (sums[0, r, f].astype(jnp.float32) + h).astype(jnp.bfloat16)
                    sums[1, r, f] = (sums[1, r, f].astype(jnp.float32) + a).astype(jnp.bfloat16)
                    chain_copy(sums, rs_send, rs_recv, d, idx, ahead).start()

                @pl.when(pos == n - 1)
                def _():
                    chain_copy(sums, rs_send, rs_recv, d, idx, behind).wait_recv()
                    hs = sums[0, r, f].astype(jnp.float32) + h
                    grad = sums[1, r, f].astype(jnp.float32) + a
                    act_full, slope = gelu_parts(hs)
                    acts[0, r, f] = act_full.astype(jnp.bfloat16)
                    acts[1, r, f] = (grad * slope).astype(jnp.bfloat16)
                    chain_copy(acts, ag_send, ag_recv, d, idx, behind).start()

            back = s - lag - (n - 1 - pos) * SKEW

            @pl.when((back >= 0) & (back < steps) & (pos < n - 1))
            def _():
                chain_copy(acts, ag_send, ag_recv, d, back, ahead).wait_recv()

                @pl.when(pos > 0)
                def _():
                    chain_copy(acts, ag_send, ag_recv, d, back, behind).start()

        done = s - 2 * lag

        @pl.when((done >= 0) & (done % per_half == per_half - 1))
        def _():
            t = block_of(done // per_half)
            r = row_slice(t)
            parts[0, r, :] = dot(acts[0, r, :], wout[...], 1, 0).astype(jnp.bfloat16)
            parts[1, r, :] = dot(acts[1, r, :], win[...], 1, 1).astype(jnp.bfloat16)
            for m in range(2):
                @pl.when((t != dp) | (my != m))
                def _():
                    out_copy(t, m, (dp, my), (t, m)).start()

    stores = [
        pltpu.make_async_copy(toks, toks_hbm, local_sem.at[0]),
        pltpu.make_async_copy(cots, cots_hbm, local_sem.at[1]),
        pltpu.make_async_copy(acts, acts_hbm, local_sem.at[2]),
    ]
    for store in stores:
        store.start()

    for d in range(2):
        pos = z if d == 0 else n - 1 - z

        @pl.loop(0, steps)
        def _(idx):
            other = jnp.where(z == 0, 1, z - 1)

            @pl.when(pos < n - 1)
            def _():
                chain_copy(sums, rs_send, rs_recv, d, idx, other).wait_send()

            @pl.when(pos > 0)
            def _():
                chain_copy(acts, ag_send, ag_recv, d, idx, other).wait_send()

    for peer in peers:
        gather_copy(0, tok_ref, toks, (dp, my), peer).wait_send()
        gather_copy(1, cot_ref, cots, (dp, my), peer).wait_send()

    out_ref[...] = parts[:, row_slice(dp), col_slice(my)].astype(jnp.float32)
    for peer in peers:
        out_copy(dp, my, peer, peer).wait_recv()
        out_ref[...] += landed[:, peer[0] * 2 + peer[1]].astype(jnp.float32)
    for peer in peers:
        out_copy(peer[0], peer[1], (dp, my), peer).wait_send()
    for store in stores:
        store.wait()


def fused(tokens, cotangent, w_in, w_out):
    n = lax.axis_size("mx")
    rows, width = tokens.shape
    hidden = w_in.shape[1] // 4
    deep = w_in.shape[0]
    bf16 = jnp.bfloat16
    steps = 4 * (hidden // 2 // TILE)
    vmem = pl.BlockSpec(memory_space=pltpu.VMEM)
    hbm = pl.BlockSpec(memory_space=pl.ANY)
    dma = pltpu.SemaphoreType.DMA
    outs, toks, cots, acts = pl.pallas_call(
        functools.partial(kernel, n),
        out_shape=(
            jax.ShapeDtypeStruct((2, rows, width), jnp.float32),
            jax.ShapeDtypeStruct((4 * rows, deep), bf16),
            jax.ShapeDtypeStruct((4 * rows, deep), bf16),
            jax.ShapeDtypeStruct((2, 4 * rows, hidden), bf16),
        ),
        in_specs=[vmem, vmem, hbm, hbm],
        out_specs=(vmem, hbm, hbm, hbm),
        scratch_shapes=[
            pltpu.VMEM((deep, hidden), bf16),
            pltpu.VMEM((hidden, deep), bf16),
            pltpu.VMEM((4 * rows, deep), bf16),
            pltpu.VMEM((4 * rows, deep), bf16),
            pltpu.VMEM((2, 4 * rows, hidden), bf16),
            pltpu.VMEM((2, 4 * rows, hidden), bf16),
            pltpu.VMEM((2, 4 * rows, deep), bf16),
            pltpu.VMEM((2, 8, rows, width), bf16),
            dma((4,)),
            dma((2, 8)),
            dma((2, 8)),
            dma((2, steps)),
            dma((2, steps)),
            dma((2, steps)),
            dma((2, steps)),
            dma((8,)),
            dma((8,)),
        ],
        compiler_params=pltpu.CompilerParams(
            collective_id=0, has_side_effects=True, vmem_limit_bytes=60 * 2**20
        ),
        cost_estimate=pl.CostEstimate(
            flops=16 * rows * hidden * deep * 2, bytes_accessed=4 * hidden * deep, transcendentals=0
        ),
    )(tokens, cotangent, w_in, w_out)
    return (
        outs[0].astype(bf16),
        outs[1].astype(bf16),
        mm(toks, acts[1], 0, 0),
        mm(acts[0], cots, 0, 0),
    )


def per_device(tokens, cotangent, w_in, w_out):
    n_dp = lax.axis_size("dp")
    aligned = tokens.shape[0] % 16 == 0 and tokens.shape[1] % 128 == 0
    aligned = aligned and w_in.shape[1] % (8 * TILE) == 0
    if n_dp == 4 and lax.axis_size("my") == 2 and lax.axis_size("mx") > 1 and aligned:
        return fused(tokens, cotangent, w_in, w_out)
    width = w_in.shape[1] // n_dp
    start = lax.axis_index("dp") * width
    win = lax.dynamic_slice_in_dim(w_in, start, width, 1)
    wout = lax.dynamic_slice_in_dim(w_out, start, width, 0)

    def gather(x):
        x = lax.all_gather(x, "my", axis=1, tiled=True)
        return lax.all_gather(x, "dp", axis=0, tiled=True)

    def scatter(x):
        x = lax.psum_scatter(x, "dp", scatter_dimension=0, tiled=True)
        return lax.psum_scatter(x, "my", scatter_dimension=1, tiled=True)

    toks = gather(tokens)
    cots = gather(cotangent)
    hidden = lax.psum_scatter(mm(toks, win, 1, 0), "mx", scatter_dimension=0, tiled=True)
    act_grad = lax.psum_scatter(mm(cots, wout, 1, 1), "mx", scatter_dimension=0, tiled=True)
    act_full, slope = gelu_parts(hidden.astype(jnp.float32))
    active = act_full.astype(jnp.bfloat16)
    hidden_grad = (act_grad.astype(jnp.float32) * slope).astype(jnp.bfloat16)
    active = lax.all_gather(active, "mx", axis=0, tiled=True)
    hidden_grad = lax.all_gather(hidden_grad, "mx", axis=0, tiled=True)
    output = scatter(mm(active, wout, 1, 0))
    input_grad = scatter(mm(hidden_grad, win, 1, 1))
    w_out_grad = mm(active, cots, 0, 0)
    w_in_grad = mm(toks, hidden_grad, 0, 0)
    return (output, input_grad, w_in_grad, w_out_grad)


def solution(mesh):
    in_specs = (P("dp", ("mx", "my")), P("dp", ("mx", "my")), P("mx", "my"), P("my", "mx"))
    out_specs = (
        P("dp", ("mx", "my")),
        P("dp", ("mx", "my")),
        P("mx", ("my", "dp")),
        P(("my", "dp"), "mx"),
    )
    return jax.shard_map(
        per_device, mesh=mesh, in_specs=in_specs, out_specs=out_specs, check_vma=False
    )
```
